128 devices in a mesh: row: 8 (over z_hi, y), col: 16 (over z_lo, x, core).
Axes of the slice: x: 4, y: 4, z: 4 (z_hi: 2, z_lo: 2; z = z_hi * 2 + z_lo), core: 2. Of those that a mesh axis runs over, the one named last changes fastest.
Arguments:
- features: bfloat16 [16, 8192, 256], P('col', 'row'), may hold values from -6 to 6
- adj_w: bfloat16 [8, 16, 320, 128, 128], P('row', 'col'), may hold values from -0.078125 to 0.078125
- row_of: int32 [8, 16, 320], P('row', 'col'), may hold values from 0 to 127
- col_of: int32 [8, 16, 320], P('row', 'col'), may hold values from 0 to 63
- live: int32 [8, 16], P('row', 'col'), may hold values from 80 to 320, as said below
- vid: int32 [8, 16384], P('row', 'col'), may hold values from 0 to 15
- w_in: bfloat16 [256, 512], replicated, may hold values from -0.375 to 0.375
- w_out: bfloat16 [512, 256], replicated, may hold values from -0.25 to 0.25
- cotangent: bfloat16 [8, 16384, 256], P('row', 'col'), may hold values from -6 to 6
Outputs:
- layer_out: bfloat16 [8, 16384, 256], P('row', 'col')
- grad_features: float32 [16, 8192, 256], P('col', 'row')
- grad_in: float32 [256, 512], replicated
- grad_out: float32 [512, 256], replicated
The draws below stay inside these ranges and needn't reach their ends.
Inputs may be any that keep to these rules, and one draw needn't show every extreme that they name: `live`: some device uses all 320 slots.
All inputs are finite; a program needn't handle non-finite values.
Results may differ from the reference program's by a relative error of at most 0.025.
Values may be sent and summed in bfloat16 or wider, within the bound.
No kernel may reach another device: no remote copies, remote signals or barrier semaphores. Data moves between devices by JAX's collectives and lax.ppermute only.
A program may use at most 192 MiB of HBM per device.

```python
import math
import jax
import jax.numpy as jnp
from jax import lax

D = 256
F = 512
VN = 16
BS = 128
BPD = 8
KDEV = 320
BR = 128
BC = 64
NODES = 131072
N_ROW = 8
N_COL = 16


def draw_live(key, part):
    key = jax.random.fold_in(key, 7)
    first, second = jax.random.split(key)
    counts = jax.random.randint(first, (N_ROW * N_COL,), KDEV // 4, KDEV + 1)
    chosen = jax.random.randint(second, (), 0, N_ROW * N_COL)
    counts = counts.at[chosen].set(KDEV)
    return counts.reshape(N_ROW, N_COL).astype(jnp.int32)


def touch_ends(entries, key, low, largest):
    dims = entries.shape
    place = [jax.random.randint(jax.random.fold_in(key, axis), (), 0, dims[axis]) for axis in range(len(dims))]
    entries = entries.at[tuple(place)].set(low)
    longest = dims.index(max(dims))
    place[longest] = (place[longest] + 1) % dims[longest]
    return entries.at[tuple(place)].set(largest)


def block_levels(stream_key, extent, shards, least, high):
    loudness, own = 1.0, jax.random.fold_in(stream_key, 6)
    for axis_at, blocks in shards:
        heights = jnp.exp(jax.random.uniform(jax.random.fold_in(own, axis_at), (blocks,), jnp.float32, least / len(shards), high / len(shards)))
        loudness = loudness * jnp.repeat(heights, extent[axis_at] // blocks).reshape([-1 if axis == axis_at else 1 for axis in range(len(extent))])
    return loudness


def normal_values(rng, extent, width, bound, cuts=(), dtype=jnp.bfloat16):
    array = width * jax.random.normal(rng, extent, jnp.float32)
    if cuts:
        array = array * block_levels(rng, extent, cuts, -0.22, 0.18)
    return jnp.clip(array, -bound, bound).astype(dtype)


def setup_inputs(seed: int = 0) -> dict:
    seeds = jax.random.split(jax.random.key(seed), 10)
    return {
        "features": normal_values(seeds[0], (N_COL, BC * BS, D), 1.0, 6.0, ((0, 16), (1, 8))),
        "adj_w": normal_values(seeds[1], (N_ROW, N_COL, KDEV, BS, BS), (BS * KDEV // BPD) ** -0.5, 0.078125, ((0, 8), (1, 16))),
        "row_of": touch_ends(jax.random.randint(seeds[2], (N_ROW, N_COL, KDEV), 0, BR), jax.random.fold_in(seeds[2], 1), 0, BR - 1).astype(jnp.int32),
        "col_of": touch_ends(jax.random.randint(seeds[3], (N_ROW, N_COL, KDEV), 0, BC), jax.random.fold_in(seeds[3], 1), 0, BC - 1).astype(jnp.int32),
        "live": draw_live(jax.random.fold_in(seeds[9], 71), 0),
        "vid": touch_ends(jax.random.randint(seeds[5], (N_ROW, BR * BS), 0, VN), jax.random.fold_in(seeds[5], 1), 0, VN - 1).astype(jnp.int32),
        "w_in": normal_values(seeds[6], (D, F), D ** -0.5, 0.375),
        "w_out": normal_values(seeds[7], (F, D), F ** -0.5, 0.25),
        "cotangent": normal_values(seeds[8], (N_ROW, BR * BS, D), 1.0, 6.0, ((0, 8), (1, 16))),
    }


def reference(features, adj_w, row_of, col_of, live, vid, w_in, w_out, cotangent):
    scale = math.sqrt(VN / NODES)
    slots = jnp.arange(KDEV)

    def forward_one(index, total):
        r = index // N_COL
        c = index % N_COL
        panel = lax.dynamic_index_in_dim(features, c, 0, keepdims=False).reshape(BC, BS, D)
        blocks = adj_w[r, c].astype(jnp.float32)
        source = panel[col_of[r, c]].astype(jnp.float32)
        prods = jnp.einsum('kij,kjd->kid', blocks, source)
        prods = prods * (slots < live[r, c]).astype(jnp.float32)[:, None, None]
        part = jax.ops.segment_sum(prods, row_of[r, c], num_segments=BR)
        part = lax.optimization_barrier(part.astype(jnp.bfloat16)).astype(jnp.float32)
        return total.at[r].add(part.reshape(BR * BS, D))
    summed = lax.fori_loop(0, N_ROW * N_COL, forward_one, jnp.zeros((N_ROW, BR * BS, D), jnp.float32))
    flat_sum = summed.reshape(NODES, D)
    ids = vid.reshape(NODES)
    pooled = scale * jax.ops.segment_sum(flat_sum, ids, num_segments=VN)
    mixed = (flat_sum + pooled[ids]).astype(jnp.bfloat16)
    pre = jnp.dot(mixed, w_in, preferred_element_type=jnp.float32)
    hidden = jax.nn.silu(pre).astype(jnp.bfloat16)
    layer_out = (jnp.dot(hidden, w_out, preferred_element_type=jnp.float32) + mixed.astype(jnp.float32)).astype(jnp.bfloat16)
    upstream = cotangent.reshape(NODES, D)
    grad_out = jnp.dot(hidden.T, upstream, preferred_element_type=jnp.float32)
    grad_hidden = jnp.dot(upstream, w_out.T, preferred_element_type=jnp.float32)
    sig = jax.nn.sigmoid(pre)
    grad_pre = (grad_hidden * sig * (1.0 + pre * (1.0 - sig))).astype(jnp.bfloat16)
    grad_in = jnp.dot(mixed.T, grad_pre, preferred_element_type=jnp.float32)
    grad_mixed = jnp.dot(grad_pre, w_in.T, preferred_element_type=jnp.float32) + upstream.astype(jnp.float32)
    grad_pooled = scale * jax.ops.segment_sum(grad_mixed, ids, num_segments=VN)
    grad_summed = (grad_mixed + grad_pooled[ids]).astype(jnp.bfloat16).reshape(N_ROW, BR, BS, D)

    def backward_one(index, total):
        r = index // N_COL
        c = index % N_COL
        panel = lax.dynamic_index_in_dim(grad_summed, r, 0, keepdims=False)
        blocks = adj_w[r, c].astype(jnp.float32)
        target = panel[row_of[r, c]].astype(jnp.float32)
        prods = jnp.einsum('kij,kid->kjd', blocks, target)
        prods = prods * (slots < live[r, c]).astype(jnp.float32)[:, None, None]
        part = jax.ops.segment_sum(prods, col_of[r, c], num_segments=BC)
        part = lax.optimization_barrier(part.astype(jnp.bfloat16)).astype(jnp.float32)
        return total.at[c].add(part.reshape(BC * BS, D))
    grad_features = lax.fori_loop(0, N_ROW * N_COL, backward_one, jnp.zeros((N_COL, BC * BS, D), jnp.float32))
    return (layer_out.reshape(N_ROW, BR * BS, D), grad_features, grad_in, grad_out)
```

```python
import functools
import math

import jax
import jax.numpy as jnp
from jax import lax
from jax.experimental import pallas as pl
from jax.experimental.pallas import tpu as pltpu
from jax.sharding import PartitionSpec as P

VN = 16
BS = 128
CHUNKS = 1
GROUP = 32
UNROLL = 4
BOTH = ("row", "col")
MIB = 1 << 20
F32, BF16 = jnp.float32, jnp.bfloat16


def route(x=0, y=0, zl=0, zh=0, core=0):
    pairs = []
    for r in range(8):
        for c in range(16):
            to_r = ((r // 4 + zh) % 2) * 4 + (r % 4 + y) % 4
            to_c = ((c // 8 + zl) % 2) * 8 + ((c // 2 % 4 + x) % 4) * 2 + (c + core) % 2
            pairs.append((r * 16 + c, to_r * 16 + to_c))
    return pairs


def send(value, **step):
    return lax.ppermute(value, BOTH, route(**step))


def along(axis):
    if axis == "row":
        return (lambda v, s: send(v, y=s)), (lambda v: send(v, zh=1))
    return (lambda v, s: send(v, x=s)), (lambda v: send(v, zl=1))


def ring_gather(axis, own):
    ring, pair = along(axis)
    half = own.shape[0] // 2
    a1, a3, b0 = ring(own, -1), ring(own, 1), pair(own)
    a2 = ring(a1[:half], -1), ring(a3[half:], 1)
    b1, b3 = ring(b0, -1), ring(b0, 1)
    b2 = ring(b1[:half], -1), ring(b3[half:], 1)
    return [own, a1, *a2, a3, b0, b1, *b2, b3]


def plus(*terms):
    total = terms[0].astype(F32)
    for term in terms[1:]:
        total = total + term.astype(F32)
    return total


def ring_sum(ring, q0, q1, q2lo, q2hi, q3):
    half = q2lo.shape[0]
    lo, hi = ring(q2lo, 1), ring(q2hi, -1)
    q1 = jnp.concatenate([plus(q1[:half], lo).astype(BF16), q1[half:]])
    q3 = jnp.concatenate([q3[:half], plus(q3[half:], hi).astype(BF16)])
    return q0, ring(q1, 1), ring(q3, -1)


def ring_scatter(axis, own, other):
    ring, pair = along(axis)
    over = pair(plus(*ring_sum(ring, *other)).astype(BF16))
    return (*ring_sum(ring, *own), over)


def everywhere(v):
    v = v + send(v, core=1)
    v = v + send(v, x=1) + send(v, x=2) + send(v, x=3)
    v = v + send(v, y=1) + send(v, y=2) + send(v, y=3)
    return v + send(v, zl=1) + send(v, zh=1) + send(v, zl=1, zh=1)


def place():
    r, c = lax.axis_index("row"), lax.axis_index("col")
    return r % 4, r // 4, c // 2 % 4, c // 8, c % 2


def sum_all(g):
    y, zh, x, zl, core = place()
    stages = [
        (2, core, lambda s: dict(core=s)),
        (4, x, lambda s: dict(x=s)),
        (4, y, lambda s: dict(y=s)),
        (4, None, None),
    ]
    z_steps = [(0, 0), (1, 0), (0, 1), (1, 1)]
    width = g.shape[1]
    for n, at, step in stages:
        parts = g.reshape(n, g.shape[0] // n, width)

        def part(s):
            if step is None:
                dl, dh = z_steps[s]
                i = ((zh + dh) % 2) * 2 + (zl + dl) % 2
            else:
                i = (at + s) % n
            return lax.dynamic_index_in_dim(parts, i, 0, keepdims=False)

        total = part(0)
        for s in range(1, n):
            to = dict(zl=z_steps[s][0], zh=z_steps[s][1]) if step is None else step(s)
            total = total + send(part(s).astype(BF16), **to).astype(F32)
        g = total
    g = g.astype(BF16)
    for n, at, step in reversed(stages):
        full = jnp.zeros((n, *g.shape), BF16)
        for s in range(n):
            if step is None:
                dl, dh = z_steps[s]
                got = g if s == 0 else send(g, zl=dl, zh=dh)
                i = ((zh + dh) % 2) * 2 + (zl + dl) % 2
            else:
                got = g if s == 0 else send(g, **step(n - s))
                i = (at + s) % n
            full = lax.dynamic_update_index_in_dim(full, got, i, 0)
        g = full.reshape(n * g.shape[0], width)
    return g


def gather_ids(vid):
    pair = jnp.stack([vid, send(vid, core=1)])
    ring = jnp.stack([pair] + [send(pair, x=4 - s) for s in range(1, 4)])
    return jnp.stack([ring, send(ring, zl=1)])


def dot(a, b, ca=1, cb=0):
    return lax.dot_general(a, b, (((ca,), (cb,)), ((), ())), preferred_element_type=F32)


def split(v):
    hi = v.astype(BF16)
    return hi, (v - hi.astype(F32)).astype(BF16)


def onehot_of(ids):
    rows = lax.broadcasted_iota(jnp.int32, (VN, ids.shape[-1]), 0)
    return (rows == ids).astype(F32).astype(BF16)


def slots_here(live_ref):
    left = jnp.clip(live_ref[0] - pl.program_id(0) * GROUP, 0, GROUP)
    return (left + UNROLL - 1) // UNROLL


def each_slot(live_ref, body):
    base = pl.program_id(0) * GROUP

    def step(i, carry):
        for u in range(UNROLL):
            body(i * UNROLL + u, base + i * UNROLL + u)
        return carry

    lax.fori_loop(0, slots_here(live_ref), step, 0)


def at_block(ref, i):
    return ref.at[pl.ds(pl.multiple_of(i * BS, BS), BS)]


def q_kernel(src, dst, live, adj, ids, out, acc):
    g = pl.program_id(0)

    @pl.when(g == 0)
    def _():
        acc[...] = jnp.zeros_like(acc)

    def slot(k, at):
        cols = pl.ds(pl.multiple_of(src[at] * BS, BS), BS)
        acc[:, cols] += dot(onehot_of(ids[dst[at]]), adj[k])

    each_slot(live, slot)

    @pl.when(g == pl.num_programs(0) - 1)
    def _():
        hi, lo = split(acc[:, : out.shape[1]])
        out[0:VN] = hi
        out[VN : 2 * VN] = lo
        out[2 * VN :] = hi


def load_panel(panel, pieces):
    row = 0
    for piece in pieces:
        panel[pl.ds(row, piece.shape[0])] = piece[...]
        row += piece.shape[0]


def store_pieces(outs, acc):
    row = 0
    for out in outs:
        out[...] = acc[pl.ds(row, out.shape[0])].astype(BF16)
        row += out.shape[0]


def forward_kernel(n_in, src, dst, live, adj, q, *refs):
    pieces, (pool, *outs), (panel, acc) = refs[:n_in], refs[n_in:-2], refs[-2:]
    g = pl.program_id(0)

    @pl.when(g == 0)
    def _():
        load_panel(panel, pieces)
        acc[...] = jnp.zeros_like(acc)
        total = jnp.zeros((2 * VN, panel.shape[1]), F32)
        deep = 1024
        for i in range(panel.shape[0] // deep):
            rows = pl.ds(i * deep, deep)
            total += dot(q[0 : 2 * VN, rows], panel[rows])
        pool[...] = total[:VN] + total[VN:]

    def slot(k, at):
        acc_at = at_block(acc, dst[at])
        acc_at[...] += dot(adj[k], at_block(panel, src[at])[...])

    each_slot(live, slot)

    @pl.when(g == pl.num_programs(0) - 1)
    def _():
        store_pieces(outs, acc)


def backward_kernel(n_in, src, dst, live, adj, q, gp, *refs):
    pieces, outs, (panel, acc) = refs[:n_in], refs[n_in:-2], refs[-2:]
    g = pl.program_id(0)

    @pl.when(g == 0)
    def _():
        load_panel(panel, pieces)
        deep = 1024
        for i in range(q.shape[1] // deep):
            rows = pl.ds(i * deep, deep)
            acc[rows] = dot(q[:, rows], gp[...], 0, 0)

    def slot(k, at):
        acc_at = at_block(acc, src[at])
        acc_at[...] += dot(adj[k], at_block(panel, dst[at])[...], 0, 0)

    each_slot(live, slot)

    @pl.when(g == pl.num_programs(0) - 1)
    def _():
        store_pieces(outs, acc)


def whole(shape):
    return pl.BlockSpec(shape, lambda *_: (0,) * len(shape), pipeline_mode=pl.Buffered(1))


def over_slots(kernel, scalars, adj, operands, out_shapes, scratch, flops):
    kslots = adj.shape[0]

    def slots(g, src, dst, live):
        last = jnp.maximum(live[0] - 1, 0) // GROUP
        return jnp.minimum(g, last), 0, 0

    return pl.pallas_call(
        kernel,
        out_shape=out_shapes,
        grid_spec=pltpu.PrefetchScalarGridSpec(
            num_scalar_prefetch=3,
            grid=(kslots // GROUP,),
            in_specs=[pl.BlockSpec((GROUP, BS, BS), slots)] + [whole(o.shape) for o in operands],
            out_specs=[whole(o.shape) for o in out_shapes],
            scratch_shapes=scratch,
        ),
        compiler_params=pltpu.CompilerParams(vmem_limit_bytes=56 * MIB),
        cost_estimate=pl.CostEstimate(flops=flops, bytes_accessed=adj.size * 2, transcendentals=0),
    )(*scalars, adj, *operands)


def mlp_kernel(n_parts, ids, pooled, w_in, w_out, cot, *refs):
    parts, (mixed_out, hidden_out, grad_pre_out, pool, *grads) = refs[:n_parts], refs[n_parts:]
    hot = onehot_of(ids[...])
    hi, lo = split(pooled[...])
    spread = dot(hot, hi, 0, 0) + dot(hot, lo, 0, 0)
    per = n_parts // len(grads)
    sums = [plus(*[p[...] for p in parts[i * per : i * per + per]]) for i in range(len(grads))]
    summed = sums[0] if len(sums) == 1 else jnp.concatenate(sums, axis=1)
    mixed = (summed + spread).astype(BF16)
    pre = dot(mixed, w_in[...])
    sig = jax.nn.sigmoid(pre)
    hidden = (pre * sig).astype(BF16)
    grad_hidden = dot(cot[...], w_out[...], 1, 1)
    grad_pre = (grad_hidden * sig * (1.0 + pre * (1.0 - sig))).astype(BF16)
    grad_mixed = dot(grad_pre, w_in[...], 1, 1) + cot[...].astype(F32)
    hi, lo = split(grad_mixed)

    @pl.when(pl.program_id(0) == 0)
    def _():
        pool[...] = jnp.zeros_like(pool)

    pool[...] += dot(hot, hi) + dot(hot, lo)
    width = hi.shape[1] // len(grads)
    for i, grad in enumerate(grads):
        grad[...] = hi[:, i * width : i * width + width]
    mixed_out[...] = mixed
    hidden_out[...] = hidden
    grad_pre_out[...] = grad_pre


def mlp(vid, pooled, w_in, w_out, cot, parts):
    rows, width = cot.shape
    hidden = w_in.shape[1]
    tile = 256
    per_row = lambda w: pl.BlockSpec((tile, w), lambda i: (i, 0))
    full = lambda a: pl.BlockSpec(a.shape, lambda i: (0, 0))
    shape = lambda w: jax.ShapeDtypeStruct((rows, w), BF16)
    return pl.pallas_call(
        functools.partial(mlp_kernel, len(parts)),
        grid=(rows // tile,),
        out_shape=[shape(width), shape(hidden), shape(hidden), jax.ShapeDtypeStruct((VN, width), F32)]
        + [shape(width // CHUNKS)] * CHUNKS,
        in_specs=[pl.BlockSpec((1, tile), lambda i: (0, i)), full(pooled), full(w_in), full(w_out), per_row(width)]
        + [per_row(width // CHUNKS)] * len(parts),
        out_specs=[per_row(width), per_row(hidden), per_row(hidden), pl.BlockSpec((VN, width), lambda i: (0, 0))]
        + [per_row(width // CHUNKS)] * CHUNKS,
        compiler_params=pltpu.CompilerParams(vmem_limit_bytes=40 * MIB),
        cost_estimate=pl.CostEstimate(
            flops=6 * rows * width * hidden, bytes_accessed=8 * rows * width, transcendentals=rows * hidden
        ),
    )(vid, pooled, w_in, w_out, cot, *parts)


def shards(features, adj_w, row_of, col_of, live, vid, w_in, w_out, cotangent):
    adj = adj_w[0, 0]
    kslots = adj.shape[0]
    nodes, width = features.shape[1:]
    owned = nodes // BS
    scale = math.sqrt(VN / (nodes * 128))
    y, zh, x, zl, core = place()
    used = jnp.arange(kslots) < live[0, 0]
    tgt, src = row_of[0, 0], col_of[0, 0]
    far = tgt // owned
    near = (((far % 2) ^ core) * 2 + ((far // 8) ^ zl)) * 4 + (far // 2 - x) % 4
    dst_blocks = 16 * owned
    src_blocks = 8 * owned
    dst = jnp.where(used, near * owned + tgt % owned, dst_blocks).astype(jnp.int32)
    home = src // owned
    at = (((home // 4) ^ zh) * 4 + (home - y) % 4) * owned + src % owned
    src = jnp.where(used, at, src_blocks).astype(jnp.int32)
    src_read = jnp.where(used, at, 0).astype(jnp.int32)
    dst_read = jnp.where(used, dst, 0)
    count = live[0]
    part = width // CHUNKS
    flops = 2 * kslots * BS * BS * part

    ids = gather_ids(vid[0])
    ids = jnp.moveaxis(ids, 2, 0).reshape(dst_blocks, 1, BS)
    (q,) = over_slots(
        q_kernel, (src, dst_read, count), adj, [ids],
        [jax.ShapeDtypeStruct((3 * VN, src_blocks * BS), BF16)],
        [pltpu.VMEM((VN, (src_blocks + 1) * BS), F32)], 2 * kslots * BS * BS * VN,
    )

    half = nodes // 2
    parts, pools = [], []
    for h in range(CHUNKS):
        pieces = ring_gather("row", features[0][:, h * part : (h + 1) * part])
        quad = jax.ShapeDtypeStruct((4 * nodes, part), BF16)
        pool, keep_w, keep_o, give_w, give_o = over_slots(
            functools.partial(forward_kernel, len(pieces)), (src_read, dst, count), adj, [q, *pieces],
            [jax.ShapeDtypeStruct((VN, part), F32)] + [quad] * 4,
            [
                pltpu.VMEM((src_blocks * BS, part), BF16),
                pltpu.VMEM(((dst_blocks + 1) * BS, part), F32),
            ],
            flops,
        )
        pools.append(pool)
        got_o, got_w = send(give_o, core=1), send(give_w, core=1)

        def cut(mine, got):
            cuts = [(0, nodes), (nodes, 2 * nodes), (2 * nodes, 2 * nodes + half), (2 * nodes + half, 3 * nodes), (3 * nodes, 4 * nodes)]
            return [plus(mine[a:b], got[a:b]).astype(BF16) for a, b in cuts]

        parts += ring_scatter("col", cut(keep_w, got_w), cut(keep_o, got_o))
    pooled = scale * everywhere(jnp.concatenate(pools, axis=1))

    mixed, hidden, grad_pre, grad_pool, *grads = mlp(vid, pooled, w_in, w_out, cotangent[0], parts)
    layer_out = (dot(hidden, w_out) + mixed.astype(F32)).astype(BF16)
    local_in = dot(grad_pre, mixed, 0, 0)
    local_out = dot(hidden, cotangent[0], 0, 0)
    grad_pooled = scale * everywhere(grad_pool)
    weights = sum_all(jnp.concatenate([local_in, local_out]))
    fan = w_in.shape[1]
    grad_in = weights[:fan].astype(F32).T
    grad_out = weights[fan:].astype(F32)

    gp_hi, gp_lo = split(grad_pooled)
    gp = jnp.concatenate([gp_hi, gp_hi, gp_lo])
    result = []
    for h in range(CHUNKS):
        pieces = ring_gather("col", grads[h])
        pieces = pieces + [send(piece, core=1) for piece in pieces]
        outs = [jax.ShapeDtypeStruct((n, part), BF16) for n in (nodes, nodes, half, half, nodes)] * 2
        sums = over_slots(
            functools.partial(backward_kernel, len(pieces)), (src, dst_read, count), adj,
            [q, gp[:, h * part : (h + 1) * part], *pieces], outs,
            [
                pltpu.VMEM((dst_blocks * BS, part), BF16),
                pltpu.VMEM(((src_blocks + 1) * BS, part), F32),
            ],
            flops,
        )
        result.append(plus(*ring_scatter("row", sums[:5], sums[5:])))
    grad_features = jnp.concatenate(result, axis=1)
    return (layer_out[None], grad_features[None], grad_in, grad_out)


def solution(mesh):
    in_specs = (
        P("col", "row", None),
        P("row", "col", None, None, None),
        P("row", "col", None),
        P("row", "col", None),
        P("row", "col"),
        P("row", "col"),
        P(),
        P(),
        P("row", "col", None),
    )
    out_specs = (P("row", "col", None), P("col", "row", None), P(), P())
    return jax.shard_map(shards, mesh=mesh, in_specs=in_specs, out_specs=out_specs, check_vma=False)
```

```python
import functools
import math

import jax
import jax.numpy as jnp
from jax import lax
from jax.experimental import pallas as pl
from jax.experimental.pallas import tpu as pltpu
from jax.sharding import PartitionSpec as P

VN = 16
BS = 128
UNROLL = 4
Q_UNROLL = 8
BOTH = ("row", "col")
MIB = 1 << 20
F32, BF16 = jnp.float32, jnp.bfloat16


def route(x=0, y=0, zl=0, zh=0, core=0):
    pairs = []
    for r in range(8):
        for c in range(16):
            to_r = ((r // 4 + zh) % 2) * 4 + (r % 4 + y) % 4
            to_c = ((c // 8 + zl) % 2) * 8 + ((c // 2 % 4 + x) % 4) * 2 + (c + core) % 2
            pairs.append((r * 16 + c, to_r * 16 + to_c))
    return pairs


def send(value, **step):
    return lax.ppermute(value, BOTH, route(**step))


def swap(value, axis, bit=1):
    stride = {"core": 1, "x": 2, "zl": 8, "y": 16, "zh": 64}[axis]
    return lax.ppermute(value, BOTH, [(i, i ^ (stride * bit)) for i in range(128)])


def tie(value, *before):
    return lax.optimization_barrier((value, before))[0]


def along(axis):
    if axis == "row":
        return (lambda v, s: send(v, y=s)), (lambda v: send(v, zh=1))
    return (lambda v, s: send(v, x=s)), (lambda v: send(v, zl=1))


def plus(*terms):
    total = terms[0].astype(F32)
    for term in terms[1:]:
        total = total + term.astype(F32)
    return total


def gather_first(axis, own):
    ring, pair = along(axis)
    return own, ring(own, -1), ring(own, 2), ring(own, 1), pair(own)


def scatter_first(axis, other):
    ring, pair = along(axis)
    return ring(other[1], 1), ring(other[3], -1), pair(other[2])


def scatter_add(own, other, got):
    r1, r3, z2 = got
    n = z2.shape[0]
    w2 = plus(own[2][:n], z2).astype(BF16)
    w2 = w2 if n == own[2].shape[0] else jnp.concatenate([w2, own[2][n:]])
    return plus(other[0], r1, r3).astype(BF16), w2


def scatter_last(axis, own, sums):
    ring, pair = along(axis)
    over, w2 = sums
    return own[0], ring(own[1], 1), ring(w2, 2), ring(own[3], -1), pair(over)


def add(value, *step):
    return value + swap(value, *step)


def place():
    r, c = lax.axis_index("row"), lax.axis_index("col")
    return r % 4, r // 4, c // 2 % 4, c // 8, c % 2


def merge(v, axis, place, bit=1):
    got = swap(v, axis, bit)
    return jnp.where(place & bit == 0, jnp.concatenate([v, got]), jnp.concatenate([got, v]))


def halve(v, place):
    n = v.shape[0] // 2
    take = lambda i: lax.dynamic_slice_in_dim(v, i * n, n)
    return take(place), take(1 - place).astype(BF16)


def agree(weights, pool, *step):
    terms = jnp.concatenate([weights.astype(BF16), *split(pool)])
    total = terms.astype(F32) + swap(terms, *step).astype(F32)
    n = weights.shape[0]
    return total[:n], total[n : n + VN] + total[n + VN :]


def dot(a, b, ca=1, cb=0):
    return lax.dot_general(a, b, (((ca,), (cb,)), ((), ())), preferred_element_type=F32)


def split(v):
    hi = v.astype(BF16)
    return hi, (v - hi.astype(F32)).astype(BF16)


def onehot_of(ids):
    rows = lax.broadcasted_iota(jnp.int32, (VN, ids.shape[-1]), 0)
    return (rows == ids).astype(F32).astype(BF16)


def fast(v):
    return pltpu.with_memory_space_constraint(v, pltpu.VMEM)


def call(kernel, scalars, operands, outs, scratch=(), flops=0, moved=0, left=0):
    vmem = pl.BlockSpec(memory_space=pltpu.VMEM)
    return pl.pallas_call(
        kernel,
        out_shape=[pltpu.VMEM(shape, dtype) for shape, dtype in outs],
        grid_spec=pltpu.PrefetchScalarGridSpec(
            num_scalar_prefetch=len(scalars),
            grid=(),
            in_specs=[pl.BlockSpec(memory_space=pl.ANY)] * left + [vmem] * (len(operands) - left),
            out_specs=[vmem] * len(outs),
            scratch_shapes=list(scratch),
        ),
        compiler_params=pltpu.CompilerParams(vmem_limit_bytes=8 * MIB),
        cost_estimate=pl.CostEstimate(flops=flops, bytes_accessed=moved, transcendentals=0),
    )(*scalars, *operands[:left], *[fast(v) for v in operands[left:]])


def slow(v):
    return pltpu.with_memory_space_constraint(v, pltpu.HBM)


def block(i):
    return pl.ds(pl.multiple_of(i * BS, BS), BS)


def q_kernel(src, dst, live, stored, ids, out, adj, acc, sems):
    parts = sems.shape[0]
    n = adj.shape[0] // parts
    copies = [pltpu.make_async_copy(stored.at[pl.ds(i * n, n)], adj.at[pl.ds(i * n, n)], sems.at[i]) for i in range(parts)]
    for copy in copies:
        copy.start()
    acc[...] = jnp.zeros_like(acc)
    for part, copy in enumerate(copies):
        copy.wait()

        def step(i, carry):
            for u in range(Q_UNROLL):
                k = part * n + i * Q_UNROLL + u
                acc[:, block(src[k])] += dot(onehot_of(ids[dst[k]]), adj[k])
            return carry

        here = jnp.clip(live[0] - part * n, 0, n)
        lax.fori_loop(0, (here + Q_UNROLL - 1) // Q_UNROLL, step, 0)
    hi, lo = split(acc[:, : out.shape[1]])
    out[0:VN] = hi
    out[VN : 2 * VN] = lo


def source_kernel(q, *refs):
    shards, (panel, pool) = refs[:8], refs[8:]
    nodes = shards[0].shape[0]
    for spot, ref in enumerate(shards):
        panel[pl.ds(spot * nodes, nodes)] = ref[...]
    panel[pl.ds(8 * nodes, BS)] = jnp.zeros((BS, panel.shape[1]), BF16)
    total = jnp.zeros((2 * VN, panel.shape[1]), F32)
    deep = 1024
    for i in range(q.shape[1] // deep):
        rows = pl.ds(i * deep, deep)
        total += dot(q[0 : 2 * VN, rows], panel[rows])
    pool[...] = total[:VN] + total[VN:]


def target_kernel(adj, *refs):
    shards, near, far, (panel, adj_out, sem, sems) = refs[:8], refs[8], refs[9:12], refs[12:]
    load = pltpu.make_async_copy(adj, adj_out, sem)
    load.start()
    nodes = shards[0].shape[0]
    moves = [(ref, 0, spot, 1) for spot, ref in enumerate(shards)] + [(near, 0, 8, 5)]
    moves += [(ref, 0, 13 + i, 1) for i, ref in enumerate(far)]
    copies = []
    for ref, at, spot, n in moves:
        to = panel.at[pl.ds(spot * nodes, n * nodes)]
        copies.append(pltpu.make_async_copy(ref.at[pl.ds(at, n * nodes)], to, sems.at[len(copies)]))
    for copy in copies:
        copy.start()
    panel[pl.ds(16 * nodes, BS)] = jnp.zeros((BS, panel.shape[1]), BF16)
    for copy in copies:
        copy.wait()
    load.wait()


def final_kernel(gp, *refs):
    terms, out = refs[:-1], refs[-1]
    hi, lo = split(gp[...])
    nodes = out.shape[0]
    width = out.shape[1]
    for k in range(nodes // width):
        rows, ride = pl.ds(k * width, width), pl.ds(nodes + k * VN, VN)
        q = plus(*[t[ride] for t in terms]).astype(BF16)
        out[rows] = plus(*[t[rows] for t in terms]) + dot(q, hi, 0, 0) + dot(q, lo, 0, 0)


def pairs_kernel(backward, low, high, c0, c1, to, ends, adj, panel, *refs):
    width = panel.shape[1]
    zero = panel.shape[0] // BS - 1
    first_pair, last = ends[low], ends[high]
    out = refs[-1]
    begin = low * (out.shape[0] // BS // (high - low))

    def step(i, acc):
        for u in range(UNROLL):
            p = first_pair + i * UNROLL + u
            real = p < last
            p = jnp.minimum(p, last - 1)
            e0, e1, t = c0[p], c1[p], to[p]
            x0 = panel[block(jnp.where(real, e0 & 255, zero))]
            x1 = panel[block(jnp.where(real, e1 & 255, zero))]
            side = 0 if backward else 1
            lhs = jnp.concatenate([adj[e0 >> 8], adj[e1 >> 8]], axis=side)
            prod = dot(lhs, jnp.concatenate([x0, x1], axis=0), side, 0)
            fresh = jnp.logical_and(real, (t & 1) == 1)
            acc = prod + jnp.where(fresh, jnp.zeros_like(acc), acc)
            out[block((t >> 1) - begin)] = acc.astype(BF16)
        return acc

    steps = (last - first_pair + UNROLL - 1) // UNROLL
    lax.fori_loop(0, steps, step, jnp.zeros((BS, width), F32))
    if backward:
        q, pieces = refs[0], refs[1:-1]
        nodes = out.shape[0] // 4
        for spot, piece in enumerate(pieces):
            piece[pl.ds(0, nodes)] = out[pl.ds(spot * nodes, nodes)]
            for k in range(nodes // width):
                piece[pl.ds(nodes + k * VN, VN)] = q[0:VN, pl.ds(((low * 4 + spot) * 4 + k) * width, width)]


def plan(used, to, frm, n_to, zero, parts):
    kslots = used.shape[0]
    n_pairs = kslots // 2 + n_to
    k = jnp.arange(kslots)
    key = jnp.where(used, to, -1)
    d = jnp.arange(n_to)
    rank = jnp.sum((key[:, None] == key[None, :]) & (k[None, :] < k[:, None]), axis=1)
    count = jnp.sum(key[None, :] == d[:, None], axis=1)
    need = jnp.maximum(1, (count + 1) // 2)
    offset = jnp.sum(jnp.where(d[None, :] < d[:, None], need[None, :], 0), axis=1)
    base = jnp.sum(jnp.where(key[:, None] == d[None, :], offset[None, :], 0), axis=1)
    spot = jnp.where(used, 2 * base + rank, -1)
    p = jnp.arange(2 * n_pairs)
    code = zero + jnp.sum(jnp.where(p[:, None] == spot[None, :], (k * 256 + frm - zero)[None, :], 0), axis=1)
    code = code.reshape(n_pairs, 2).astype(jnp.int32)
    p = jnp.arange(n_pairs)
    at = jnp.sum(offset[None, :] <= p[:, None], axis=1) - 1
    first = jnp.sum(offset[None, :] == p[:, None], axis=1)
    ends = jnp.stack([offset[i * n_to // parts] for i in range(parts)] + [jnp.sum(need)]).astype(jnp.int32)
    return code[:, 0], code[:, 1], (2 * at + first).astype(jnp.int32), ends


def mlp_kernel(ids, pooled, w_in, w_out, cot, *refs):
    terms, (mixed_out, hidden_out, grad_pre_out, grad, pool) = refs[:5], refs[5:]
    p_hi, p_lo = split(pooled[...])
    tile = 256
    total = jnp.zeros(pooled.shape, F32)
    for i in range(cot.shape[0] // tile):
        rows = pl.ds(i * tile, tile)
        hot = onehot_of(ids[:, rows])
        spread = dot(hot, p_hi, 0, 0) + dot(hot, p_lo, 0, 0)
        mixed = (plus(*[t[rows] for t in terms]) + spread).astype(BF16)
        pre = dot(mixed, w_in[...])
        sig = jax.nn.sigmoid(pre)
        hidden_out[rows] = (pre * sig).astype(BF16)
        grad_hidden = dot(cot[rows], w_out[...], 1, 1)
        grad_pre = (grad_hidden * sig * (1.0 + pre * (1.0 - sig))).astype(BF16)
        hi, lo = split(dot(grad_pre, w_in[...], 1, 1) + cot[rows].astype(F32))
        total += dot(hot, hi) + dot(hot, lo)
        grad[rows] = hi
        mixed_out[rows] = mixed
        grad_pre_out[rows] = grad_pre
    pool[pl.ds(0, VN)], pool[pl.ds(VN, VN)] = split(total)


def mlp(vid, pooled, w_in, w_out, cot, parts):
    rows, width = cot.shape
    hidden = w_in.shape[1]
    return call(
        mlp_kernel, (), [vid, pooled, w_in, w_out, cot, *parts],
        [((rows, width), BF16), ((rows, hidden), BF16), ((rows, hidden), BF16), ((rows, width), BF16), ((2 * VN, width), BF16)],
        (), 6 * rows * width * hidden, 8 * rows * width,
    )


def shards(features, adj_w, row_of, col_of, live, vid, w_in, w_out, cotangent):
    adj = adj_w[0, 0]
    kslots = adj.shape[0]
    nodes, width = features.shape[1:]
    owned = nodes // BS
    scale = math.sqrt(VN / (nodes * 128))
    y, zh, x, zl, core = place()
    used = jnp.arange(kslots) < live[0, 0]
    tgt, src = row_of[0, 0], col_of[0, 0]
    far = tgt // owned
    near = (((far % 2) ^ core) * 2 + ((far // 8) ^ zl)) * 4 + (far // 2 - x) % 4
    dst_blocks = 16 * owned
    src_blocks = 8 * owned
    dst = jnp.where(used, near * owned + tgt % owned, dst_blocks).astype(jnp.int32)
    home = src // owned
    at = (((home // 4) ^ zh) * 4 + (home - y) % 4) * owned + src % owned
    src = jnp.where(used, at, src_blocks).astype(jnp.int32)
    tgt_read = jnp.where(used, tgt, 0)
    count = live[0]
    to_dst = plan(used, dst, src, dst_blocks, src_blocks, 4)
    to_src = plan(used, src, dst, src_blocks, dst_blocks, 2)
    part = width
    flops = 2 * kslots * BS * BS * part

    ring, pair = along("row")
    own, a1, a2, a3, b0 = gather_first("row", features[0])
    stored = slow(adj)
    ids = merge(merge(vid[0][None], "core", core), "x", x, 1)
    ids = merge(merge(ids, "x", x, 2), "zl", zl).reshape(dst_blocks, 1, BS)
    a2, ids = tie((a2, ids), to_dst, to_src)
    b1, b2, b3 = ring(b0, -1), pair(a2), ring(b0, 1)
    q, adj = call(
        q_kernel, (src, tgt_read, count), [stored, ids], [((2 * VN, src_blocks * BS), BF16), (adj.shape, BF16)],
        [pltpu.VMEM((VN, (src_blocks + 1) * BS), F32), pltpu.SemaphoreType.DMA((5,))],
        2 * kslots * BS * BS * VN, adj.size * 2, 1,
    )
    pieces = [own, a1, a2, a3, b0, *tie((b1, b2, b3), q)]
    panel, pool = call(
        source_kernel, (), [q, *pieces], [(((src_blocks + 1) * BS, part), BF16), ((VN, part), F32)]
    )

    def forward(low, high, panel):
        return call(
            functools.partial(pairs_kernel, False, low, high), to_dst, [adj, panel],
            [((dst_blocks // 4 * (high - low) * BS, part), BF16)], (), flops // 2, adj.size,
        )[0]

    give = forward(2, 4, panel)
    pool, panel = tie((add(pool, "zl"), panel), give)
    got = send(give, core=1)
    keep_o = forward(1, 2, panel)
    pool, keep_o = tie((add(pool, "zh"), keep_o))
    piece = lambda keep, at, i: plus(keep[i * nodes : i * nodes + nodes], got[(at + i) * nodes : (at + i + 1) * nodes]).astype(BF16)
    other = [piece(keep_o, 4, i) for i in range(4)]
    o = scatter_first("col", other)
    pool, panel = tie((pool, panel), other)
    keep_w = forward(0, 1, panel)
    pool, keep_w = tie((add(pool, "y"), keep_w))
    pool, keep_w, o = tie((add(add(pool, "y", 2), "core"), keep_w, o))
    rider = jnp.concatenate(split(pool))
    own = [jnp.concatenate([piece(keep_w, 0, i), rider]) for i in range(4)]
    parts = scatter_last("col", own, scatter_add(own, other, o))
    riders = [p[nodes:] for p in parts[:4]]
    pooled = scale * plus(*[r[:VN] for r in riders], *[r[VN:] for r in riders])

    mixed, hidden, grad_pre, grad, pool = mlp(vid, pooled, w_in, w_out, cotangent[0], parts)
    ring, pair = along("col")
    own, a1, a2, a3, b0 = gather_first("col", grad)
    weights = jnp.concatenate([dot(grad_pre, mixed, 0, 0), dot(hidden, cotangent[0], 0, 0)])
    layer_out = (dot(hidden, w_out) + mixed.astype(F32)).astype(BF16)
    fan = w_in.shape[1]
    quads = weights.reshape(4, fan // 2, width)
    w0, w1, w2, w3 = [lax.dynamic_index_in_dim(quads, (x + k) % 4, 0, keepdims=False).astype(BF16) for k in range(4)]
    a2, b0 = tie((a2, b0), layer_out, w1, w2, w3)
    b1 = ring(jnp.concatenate([b0, w3, pool]), -1)
    b3 = ring(jnp.concatenate([b0, w1, pool]), 1)
    b2 = pair(a2)
    near = send(jnp.concatenate([own, a1, a2, a3, b0]), core=1)
    terms = jnp.concatenate([w0, pool]), ring(jnp.concatenate([w2, pool]), 2), b1[nodes:], b3[nodes:]
    terms = plus(*terms)
    deep = fan // 2
    weights, pool = terms[:deep], terms[deep : deep + VN] + terms[deep + VN :]
    far = [send(b, core=1) for b in (b1, b2, b3)]
    weights, pool = agree(weights, pool, "y")
    panel, adj = call(
        target_kernel, (), [stored, own, a1, a2, a3, b0, b1, b2, b3, near, *far],
        [(((dst_blocks + 1) * BS, part), BF16), (stored.shape, BF16)],
        [pltpu.SemaphoreType.DMA, pltpu.SemaphoreType.DMA((12,))], 0, stored.size * 2, 13,
    )
    weights, pool, panel = tie((weights, pool, panel))

    ride = nodes // width * VN
    outs = [((nodes + ride, part), BF16)] * 4

    def backward(low, panel):
        return call(
            functools.partial(pairs_kernel, True, low, low + 1), to_src, [adj, panel, q],
            outs, [pltpu.VMEM((src_blocks // 2 * BS, part), BF16)], flops // 2, adj.size,
        )

    other = backward(1, panel)
    weights, pool, other = tie((*agree(weights, pool, "zh"), other))
    o = scatter_first("row", other)
    own = backward(0, panel)
    weights, pool, own, o = tie((*agree(weights, pool, "y", 2), own, o))
    sums = scatter_add(own, other, o)
    weights, pool = tie((weights, pool), sums)
    terms = scatter_last("row", own, sums)
    weights, pool = agree(*agree(weights, pool, "core"), "zl")
    weights = tie(weights.astype(BF16), terms[-1])
    for bit in (1, 2):
        weights = merge(weights, "x", x, bit)
    grad_features = pl.pallas_call(
        final_kernel, out_shape=jax.ShapeDtypeStruct((nodes, part), F32)
    )(scale * pool, *terms)
    grad_in = weights[:fan].astype(F32).T
    grad_out = weights[fan:].astype(F32)
    return (layer_out[None], grad_features[None], grad_in, grad_out)


def solution(mesh):
    in_specs = (
        P("col", "row", None),
        P("row", "col", None, None, None),
        P("row", "col", None),
        P("row", "col", None),
        P("row", "col"),
        P("row", "col"),
        P(),
        P(),
        P("row", "col", None),
    )
    out_specs = (P("row", "col", None), P("col", "row", None), P(), P())
    return jax.shard_map(shards, mesh=mesh, in_specs=in_specs, out_specs=out_specs, check_vma=False)
```

```python
import functools
import math

import jax
import jax.numpy as jnp
from jax import lax
from jax.experimental import pallas as pl
from jax.experimental.pallas import tpu as pltpu
from jax.sharding import PartitionSpec as P

VN = 16
BS = 128
UNROLL = 4
Q_UNROLL = 8
BOTH = ("row", "col")
MIB = 1 << 20
F32, BF16 = jnp.float32, jnp.bfloat16


def route(x=0, y=0, zl=0, zh=0, core=0):
    pairs = []
    for r in range(8):
        for c in range(16):
            to_r = ((r // 4 + zh) % 2) * 4 + (r % 4 + y) % 4
            to_c = ((c // 8 + zl) % 2) * 8 + ((c // 2 % 4 + x) % 4) * 2 + (c + core) % 2
            pairs.append((r * 16 + c, to_r * 16 + to_c))
    return pairs


def send(value, **step):
    return lax.ppermute(value, BOTH, route(**step))


def swap(value, axis, bit=1):
    stride = {"core": 1, "x": 2, "zl": 8, "y": 16, "zh": 64}[axis]
    return lax.ppermute(value, BOTH, [(i, i ^ (stride * bit)) for i in range(128)])


def tie(value, *before):
    return lax.optimization_barrier((value, before))[0]


def along(axis):
    if axis == "row":
        return (lambda v, s: send(v, y=s)), (lambda v: send(v, zh=1))
    return (lambda v, s: send(v, x=s)), (lambda v: send(v, zl=1))


def plus(*terms):
    total = terms[0].astype(F32)
    for term in terms[1:]:
        total = total + term.astype(F32)
    return total


def gather_first(axis, own):
    ring, pair = along(axis)
    return own, ring(own, -1), ring(own, 2), ring(own, 1), pair(own)


def scatter_first(axis, other):
    ring, pair = along(axis)
    return ring(other[1], 1), ring(other[3], -1), pair(other[2])


def scatter_add(own, other, got):
    r1, r3, z2 = got
    n = z2.shape[0]
    w2 = plus(own[2][:n], z2).astype(BF16)
    w2 = w2 if n == own[2].shape[0] else jnp.concatenate([w2, own[2][n:]])
    return plus(other[0], r1, r3).astype(BF16), w2


def scatter_last(axis, own, sums):
    ring, pair = along(axis)
    over, w2 = sums
    return own[0], ring(own[1], 1), ring(w2, 2), ring(own[3], -1), pair(over)


def add(value, *step):
    return value + swap(value, *step)


def place():
    r, c = lax.axis_index("row"), lax.axis_index("col")
    return r % 4, r // 4, c // 2 % 4, c // 8, c % 2


def merge(v, axis, place, bit=1):
    got = swap(v, axis, bit)
    return jnp.where(place & bit == 0, jnp.concatenate([v, got]), jnp.concatenate([got, v]))


def halve(v, place):
    n = v.shape[0] // 2
    take = lambda i: lax.dynamic_slice_in_dim(v, i * n, n)
    return take(place), take(1 - place).astype(BF16)


def as_sent(weights, pool):
    return jnp.concatenate([weights.astype(BF16), *split(pool)])


def as_held(total):
    n = total.shape[0] - 2 * VN
    return total[:n], total[n : n + VN] + total[n + VN :]


def agree(weights, pool, beside, *step):
    terms = as_sent(weights, pool)
    return as_held(plus(terms, tie(swap(terms, *step), beside)))


def dot(a, b, ca=1, cb=0):
    return lax.dot_general(a, b, (((ca,), (cb,)), ((), ())), preferred_element_type=F32)


def split(v):
    hi = v.astype(BF16)
    return hi, (v - hi.astype(F32)).astype(BF16)


def onehot_of(ids):
    rows = lax.broadcasted_iota(jnp.int32, (VN, ids.shape[-1]), 0)
    return (rows == ids).astype(F32).astype(BF16)


def fast(v):
    return pltpu.with_memory_space_constraint(v, pltpu.VMEM)


def call(kernel, scalars, operands, outs, scratch=(), flops=0, moved=0, left=0):
    vmem = pl.BlockSpec(memory_space=pltpu.VMEM)
    return pl.pallas_call(
        kernel,
        out_shape=[pltpu.VMEM(shape, dtype) for shape, dtype in outs],
        grid_spec=pltpu.PrefetchScalarGridSpec(
            num_scalar_prefetch=len(scalars),
            grid=(),
            in_specs=[pl.BlockSpec(memory_space=pl.ANY)] * left + [vmem] * (len(operands) - left),
            out_specs=[vmem] * len(outs),
            scratch_shapes=list(scratch),
        ),
        compiler_params=pltpu.CompilerParams(vmem_limit_bytes=8 * MIB),
        cost_estimate=pl.CostEstimate(flops=flops, bytes_accessed=moved, transcendentals=0),
    )(*scalars, *operands[:left], *[fast(v) for v in operands[left:]])


def slow(v):
    return pltpu.with_memory_space_constraint(v, pltpu.HBM)


def block(i):
    return pl.ds(pl.multiple_of(i * BS, BS), BS)


def q_kernel(src, dst, live, stored, ids, out, adj, acc, sems):
    parts = sems.shape[0]
    n = adj.shape[0] // parts
    copies = [pltpu.make_async_copy(stored.at[pl.ds(i * n, n)], adj.at[pl.ds(i * n, n)], sems.at[i]) for i in range(parts)]
    for copy in copies:
        copy.start()
    acc[...] = jnp.zeros_like(acc)
    for part, copy in enumerate(copies):
        copy.wait()

        def step(i, carry):
            for u in range(Q_UNROLL):
                k = part * n + i * Q_UNROLL + u
                acc[:, block(src[k])] += dot(onehot_of(ids[dst[k]]), adj[k])
            return carry

        here = jnp.clip(live[0] - part * n, 0, n)
        lax.fori_loop(0, (here + Q_UNROLL - 1) // Q_UNROLL, step, 0)
    hi, lo = split(acc[:, : out.shape[1]])
    out[0:VN] = hi
    out[VN : 2 * VN] = lo


def source_kernel(q, *refs):
    shards, (panel, pool) = refs[:8], refs[8:]
    nodes = shards[0].shape[0]
    for spot, ref in enumerate(shards):
        panel[pl.ds(spot * nodes, nodes)] = ref[...]
    panel[pl.ds(8 * nodes, BS)] = jnp.zeros((BS, panel.shape[1]), BF16)
    total = jnp.zeros((2 * VN, panel.shape[1]), F32)
    deep = 1024
    for i in range(q.shape[1] // deep):
        rows = pl.ds(i * deep, deep)
        total += dot(q[0 : 2 * VN, rows], panel[rows])
    pool[...] = total[:VN] + total[VN:]


def target_kernel(adj, *refs):
    shards, near, far, (panel, adj_out, sem, sems) = refs[:8], refs[8], refs[9:12], refs[12:]
    load = pltpu.make_async_copy(adj, adj_out, sem)
    load.start()
    nodes = shards[0].shape[0]
    moves = [(ref, 0, spot, 1) for spot, ref in enumerate(shards)] + [(near, 0, 8, 5)]
    moves += [(ref, 0, 13 + i, 1) for i, ref in enumerate(far)]
    copies = []
    for ref, at, spot, n in moves:
        to = panel.at[pl.ds(spot * nodes, n * nodes)]
        copies.append(pltpu.make_async_copy(ref.at[pl.ds(at, n * nodes)], to, sems.at[len(copies)]))
    for copy in copies:
        copy.start()
    panel[pl.ds(16 * nodes, BS)] = jnp.zeros((BS, panel.shape[1]), BF16)
    for copy in copies:
        copy.wait()
    load.wait()


def final_kernel(gp, *refs):
    terms, out = refs[:-1], refs[-1]
    hi, lo = split(gp[...])
    nodes = out.shape[0]
    width = out.shape[1]
    for k in range(nodes // width):
        rows, ride = pl.ds(k * width, width), pl.ds(nodes + k * VN, VN)
        q = plus(*[t[ride] for t in terms]).astype(BF16)
        out[rows] = plus(*[t[rows] for t in terms]) + dot(q, hi, 0, 0) + dot(q, lo, 0, 0)


def pairs_kernel(backward, low, high, c0, c1, to, ends, adj, panel, *refs):
    width = panel.shape[1]
    zero = panel.shape[0] // BS - 1
    first_pair, last = ends[low], ends[high]
    out = refs[-1]
    begin = low * (out.shape[0] // BS // (high - low))

    def step(i, acc):
        for u in range(UNROLL):
            p = first_pair + i * UNROLL + u
            real = p < last
            p = jnp.minimum(p, last - 1)
            e0, e1, t = c0[p], c1[p], to[p]
            x0 = panel[block(jnp.where(real, e0 & 255, zero))]
            x1 = panel[block(jnp.where(real, e1 & 255, zero))]
            side = 0 if backward else 1
            lhs = jnp.concatenate([adj[e0 >> 8], adj[e1 >> 8]], axis=side)
            prod = dot(lhs, jnp.concatenate([x0, x1], axis=0), side, 0)
            fresh = jnp.logical_and(real, (t & 1) == 1)
            acc = prod + jnp.where(fresh, jnp.zeros_like(acc), acc)
            out[block((t >> 1) - begin)] = acc.astype(BF16)
        return acc

    steps = (last - first_pair + UNROLL - 1) // UNROLL
    lax.fori_loop(0, steps, step, jnp.zeros((BS, width), F32))
    if backward:
        q, pieces = refs[0], refs[1:-1]
        nodes = out.shape[0] // 4
        for spot, piece in enumerate(pieces):
            piece[pl.ds(0, nodes)] = out[pl.ds(spot * nodes, nodes)]
            for k in range(nodes // width):
                piece[pl.ds(nodes + k * VN, VN)] = q[0:VN, pl.ds(((low * 4 + spot) * 4 + k) * width, width)]


def plan(used, to, frm, n_to, zero, parts):
    kslots = used.shape[0]
    n_pairs = kslots // 2 + n_to
    k = jnp.arange(kslots)
    key = jnp.where(used, to, -1)
    d = jnp.arange(n_to)
    rank = jnp.sum((key[:, None] == key[None, :]) & (k[None, :] < k[:, None]), axis=1)
    count = jnp.sum(key[None, :] == d[:, None], axis=1)
    need = jnp.maximum(1, (count + 1) // 2)
    offset = jnp.sum(jnp.where(d[None, :] < d[:, None], need[None, :], 0), axis=1)
    base = jnp.sum(jnp.where(key[:, None] == d[None, :], offset[None, :], 0), axis=1)
    spot = jnp.where(used, 2 * base + rank, -1)
    p = jnp.arange(2 * n_pairs)
    code = zero + jnp.sum(jnp.where(p[:, None] == spot[None, :], (k * 256 + frm - zero)[None, :], 0), axis=1)
    code = code.reshape(n_pairs, 2).astype(jnp.int32)
    p = jnp.arange(n_pairs)
    at = jnp.sum(offset[None, :] <= p[:, None], axis=1) - 1
    first = jnp.sum(offset[None, :] == p[:, None], axis=1)
    ends = jnp.stack([offset[i * n_to // parts] for i in range(parts)] + [jnp.sum(need)]).astype(jnp.int32)
    return code[:, 0], code[:, 1], (2 * at + first).astype(jnp.int32), ends


def mlp_kernel(ids, pooled, w_in, w_out, cot, *refs):
    terms, (mixed_out, hidden_out, grad_pre_out, grad, pool) = refs[:5], refs[5:]
    p_hi, p_lo = split(pooled[...])
    tile = 256
    total = jnp.zeros(pooled.shape, F32)
    for i in range(cot.shape[0] // tile):
        rows = pl.ds(i * tile, tile)
        hot = onehot_of(ids[:, rows])
        spread = dot(hot, p_hi, 0, 0) + dot(hot, p_lo, 0, 0)
        mixed = (plus(*[t[rows] for t in terms]) + spread).astype(BF16)
        pre = dot(mixed, w_in[...])
        sig = jax.nn.sigmoid(pre)
        hidden_out[rows] = (pre * sig).astype(BF16)
        grad_hidden = dot(cot[rows], w_out[...], 1, 1)
        grad_pre = (grad_hidden * sig * (1.0 + pre * (1.0 - sig))).astype(BF16)
        hi, lo = split(dot(grad_pre, w_in[...], 1, 1) + cot[rows].astype(F32))
        total += dot(hot, hi) + dot(hot, lo)
        grad[rows] = hi
        mixed_out[rows] = mixed
        grad_pre_out[rows] = grad_pre
    pool[pl.ds(0, VN)], pool[pl.ds(VN, VN)] = split(total)


def mlp(vid, pooled, w_in, w_out, cot, parts):
    rows, width = cot.shape
    hidden = w_in.shape[1]
    return call(
        mlp_kernel, (), [vid, pooled, w_in, w_out, cot, *parts],
        [((rows, width), BF16), ((rows, hidden), BF16), ((rows, hidden), BF16), ((rows, width), BF16), ((2 * VN, width), BF16)],
        (), 6 * rows * width * hidden, 8 * rows * width,
    )


def shards(features, adj_w, row_of, col_of, live, vid, w_in, w_out, cotangent):
    adj = adj_w[0, 0]
    kslots = adj.shape[0]
    nodes, width = features.shape[1:]
    owned = nodes // BS
    scale = math.sqrt(VN / (nodes * 128))
    y, zh, x, zl, core = place()
    used = jnp.arange(kslots) < live[0, 0]
    tgt, src = row_of[0, 0], col_of[0, 0]
    far = tgt // owned
    near = (((far % 2) ^ core) * 2 + ((far // 8) ^ zl)) * 4 + (far // 2 - x) % 4
    dst_blocks = 16 * owned
    src_blocks = 8 * owned
    dst = jnp.where(used, near * owned + tgt % owned, dst_blocks).astype(jnp.int32)
    home = src // owned
    at = (((home // 4) ^ zh) * 4 + (home - y) % 4) * owned + src % owned
    src = jnp.where(used, at, src_blocks).astype(jnp.int32)
    tgt_read = jnp.where(used, tgt, 0)
    count = live[0]
    to_dst = plan(used, dst, src, dst_blocks, src_blocks, 4)
    to_src = plan(used, src, dst, src_blocks, dst_blocks, 2)
    part = width
    flops = 2 * kslots * BS * BS * part

    ring, pair = along("row")
    own, a1, a2, a3, b0 = gather_first("row", features[0])
    stored = slow(adj)
    ids = merge(merge(vid[0][None], "core", core), "x", x, 1)
    ids = merge(merge(ids, "x", x, 2), "zl", zl).reshape(dst_blocks, 1, BS)
    a2, ids = tie((a2, ids))
    b1, b2, b3 = ring(b0, -1), pair(a2), ring(b0, 1)
    ids = tie(ids, to_dst, to_src)
    q, adj = call(
        q_kernel, (src, tgt_read, count), [stored, ids], [((2 * VN, src_blocks * BS), BF16), (adj.shape, BF16)],
        [pltpu.VMEM((VN, (src_blocks + 1) * BS), F32), pltpu.SemaphoreType.DMA((5,))],
        2 * kslots * BS * BS * VN, adj.size * 2, 1,
    )
    pieces = [own, a1, a2, a3, b0, *tie((b1, b2, b3), q)]
    panel, pool = call(
        source_kernel, (), [q, *pieces], [(((src_blocks + 1) * BS, part), BF16), ((VN, part), F32)]
    )

    def forward(low, high, panel):
        return call(
            functools.partial(pairs_kernel, False, low, high), to_dst, [adj, panel],
            [((dst_blocks // 4 * (high - low) * BS, part), BF16)], (), flops // 2, adj.size,
        )[0]

    give = forward(2, 4, panel)
    pool, panel = tie((add(pool, "zl"), panel), give)
    got = send(give, core=1)
    keep_o = forward(1, 2, panel)
    pool, keep_o = tie((add(pool, "zh"), keep_o))
    piece = lambda keep, at, i: plus(keep[i * nodes : i * nodes + nodes], got[(at + i) * nodes : (at + i + 1) * nodes]).astype(BF16)
    other = [piece(keep_o, 4, i) for i in range(4)]
    o = scatter_first("col", other)
    pool, panel = tie((pool, panel), other)
    keep_w = forward(0, 1, panel)
    pool, keep_w = tie((add(pool, "y"), keep_w))
    pool, keep_w, o = tie((add(add(pool, "y", 2), "core"), keep_w, o))
    rider = jnp.concatenate(split(pool))
    own = [jnp.concatenate([piece(keep_w, 0, i), rider]) for i in range(4)]
    parts = scatter_last("col", own, scatter_add(own, other, o))
    riders = [p[nodes:] for p in parts[:4]]
    pooled = scale * plus(*[r[:VN] for r in riders], *[r[VN:] for r in riders])

    mixed, hidden, grad_pre, grad, pool = mlp(vid, pooled, w_in, w_out, cotangent[0], parts)
    ring, pair = along("col")
    own, a1, a2, a3, b0 = gather_first("col", grad)
    weights = jnp.concatenate([dot(grad_pre, mixed, 0, 0), dot(hidden, cotangent[0], 0, 0)])
    layer_out = (dot(hidden, w_out) + mixed.astype(F32)).astype(BF16)
    fan = w_in.shape[1]
    weights, pool = agree(weights, as_held(pool.astype(F32))[1], layer_out, "zl")
    quads = weights.reshape(4, fan // 2, width)
    pool = jnp.concatenate(split(pool))
    w0, w1, w2, w3 = [lax.dynamic_index_in_dim(quads, (x + k) % 4, 0, keepdims=False).astype(BF16) for k in range(4)]
    b0 = tie(b0, layer_out)
    a2 = tie(a2, w2)
    b1 = ring(jnp.concatenate([b0, w3, pool]), -1)
    b3 = ring(jnp.concatenate([b0, w1, pool]), 1)
    b2 = pair(a2)
    near = send(jnp.concatenate([own, a1, a2, a3, b0]), core=1)
    terms = jnp.concatenate([w0, pool]), ring(jnp.concatenate([w2, pool]), 2), b1[nodes:], b3[nodes:]
    terms = as_sent(*as_held(plus(*terms)))
    far = [send(b, core=1) for b in (b1, jnp.concatenate([b2, terms]), b3)]
    weights, pool = as_held(plus(terms, far[1][nodes:]))
    panel, adj = call(
        target_kernel, (), [stored, own, a1, a2, a3, b0, b1, b2, b3, near, *far],
        [(((dst_blocks + 1) * BS, part), BF16), (stored.shape, BF16)],
        [pltpu.SemaphoreType.DMA, pltpu.SemaphoreType.DMA((12,))], 0, stored.size * 2, 13,
    )
    weights, pool, panel = tie((*agree(weights, pool, panel, "y", 2), panel))

    ride = nodes // width * VN
    outs = [((nodes + ride, part), BF16)] * 4

    def backward(low, panel):
        return call(
            functools.partial(pairs_kernel, True, low, low + 1), to_src, [adj, panel, q],
            outs, [pltpu.VMEM((src_blocks // 2 * BS, part), BF16)], flops // 2, adj.size,
        )

    other = backward(1, panel)
    weights, pool, other = tie((*agree(weights, pool, other, "y"), other))
    o = scatter_first("row", other)
    own = backward(0, panel)
    weights, pool, own, o = tie((*agree(weights, pool, (own, o), "zh"), own, o))
    terms = scatter_last("row", own, scatter_add(own, other, o))
    weights = tie(weights.astype(BF16), terms[-1])
    for bit in (1, 2):
        weights = merge(weights, "x", x, bit)
    grad_in = weights[:fan].astype(F32).T
    grad_out = weights[fan:].astype(F32)
    grad_features = pl.pallas_call(
        final_kernel, out_shape=jax.ShapeDtypeStruct((nodes, part), F32)
    )(scale * pool, *[fast(t) for t in terms])
    return (layer_out[None], grad_features[None], grad_in, grad_out)


def solution(mesh):
    in_specs = (
        P("col", "row", None),
        P("row", "col", None, None, None),
        P("row", "col", None),
        P("row", "col", None),
        P("row", "col"),
        P("row", "col"),
        P(),
        P(),
        P("row", "col", None),
    )
    out_specs = (P("row", "col", None), P("col", "row", None), P(), P())
    return jax.shard_map(shards, mesh=mesh, in_specs=in_specs, out_specs=out_specs, check_vma=False)
```

```python
import functools
import math

import jax
import jax.numpy as jnp
from jax import lax
from jax.experimental import pallas as pl
from jax.experimental.pallas import tpu as pltpu
from jax.sharding import PartitionSpec as P

VN = 16
BS = 128
UNROLL = 16
Q_UNROLL = 16
BOTH = ("row", "col")
MIB = 1 << 20
F32, BF16 = jnp.float32, jnp.bfloat16


def route(x=0, y=0, zl=0, zh=0, core=0):
    pairs = []
    for r in range(8):
        for c in range(16):
            to_r = ((r // 4 + zh) % 2) * 4 + (r % 4 + y) % 4
            to_c = ((c // 8 + zl) % 2) * 8 + ((c // 2 % 4 + x) % 4) * 2 + (c + core) % 2
            pairs.append((r * 16 + c, to_r * 16 + to_c))
    return pairs


def send(value, **step):
    return lax.ppermute(value, BOTH, route(**step))


def swap(value, axis, bit=1):
    stride = {"core": 1, "x": 2, "zl": 8, "y": 16, "zh": 64}[axis]
    return lax.ppermute(value, BOTH, [(i, i ^ (stride * bit)) for i in range(128)])


def tie(value, *before):
    return lax.optimization_barrier((value, before))[0]


def along(axis):
    if axis == "row":
        return (lambda v, s: send(v, y=s)), (lambda v: send(v, zh=1))
    return (lambda v, s: send(v, x=s)), (lambda v: send(v, zl=1))


def plus(*terms):
    total = terms[0].astype(F32)
    for term in terms[1:]:
        total = total + term.astype(F32)
    return total


def gather_first(axis, own):
    ring, pair = along(axis)
    return own, ring(own, -1), ring(own, 2), ring(own, 1), pair(own)


def scatter_first(axis, other):
    ring, pair = along(axis)
    return ring(other[1], 1), ring(other[3], -1), pair(other[2])


def scatter_add(own, other, got):
    r1, r3, z2 = got
    n = z2.shape[0]
    w2 = plus(own[2][:n], z2).astype(BF16)
    w2 = w2 if n == own[2].shape[0] else jnp.concatenate([w2, own[2][n:]])
    return plus(other[0], r1, r3).astype(BF16), w2


def scatter_last(axis, own, sums):
    ring, pair = along(axis)
    over, w2 = sums
    return own[0], ring(own[1], 1), ring(w2, 2), ring(own[3], -1), pair(over)


def add(value, *step):
    return value + swap(value, *step)


def place():
    r, c = lax.axis_index("row"), lax.axis_index("col")
    return r % 4, r // 4, c // 2 % 4, c // 8, c % 2


def merge(v, axis, place, bit=1):
    got = swap(v, axis, bit)
    return jnp.where(place & bit == 0, jnp.concatenate([v, got]), jnp.concatenate([got, v]))


def halve(v, place):
    n = v.shape[0] // 2
    take = lambda i: lax.dynamic_slice_in_dim(v, i * n, n)
    return take(place), take(1 - place).astype(BF16)


def as_sent(weights, pool):
    return jnp.concatenate([weights.astype(BF16), *split(pool)])


def as_held(total):
    n = total.shape[0] - 2 * VN
    return total[:n], total[n : n + VN] + total[n + VN :]


def agree(weights, pool, beside, *step):
    terms = as_sent(weights, pool)
    return as_held(plus(terms, tie(swap(terms, *step), beside)))


def dot(a, b, ca=1, cb=0):
    return lax.dot_general(a, b, (((ca,), (cb,)), ((), ())), preferred_element_type=F32)


def split(v):
    hi = v.astype(BF16)
    return hi, (v - hi.astype(F32)).astype(BF16)


def onehot_of(ids):
    rows = lax.broadcasted_iota(jnp.int32, (VN, ids.shape[-1]), 0)
    return (rows == ids).astype(F32).astype(BF16)


def fast(v):
    return pltpu.with_memory_space_constraint(v, pltpu.VMEM)


def call(kernel, scalars, operands, outs, scratch=(), flops=0, moved=0, left=0):
    vmem = pl.BlockSpec(memory_space=pltpu.VMEM)
    return pl.pallas_call(
        kernel,
        out_shape=[pltpu.VMEM(shape, dtype) for shape, dtype in outs],
        grid_spec=pltpu.PrefetchScalarGridSpec(
            num_scalar_prefetch=len(scalars),
            grid=(),
            in_specs=[pl.BlockSpec(memory_space=pl.ANY)] * left + [vmem] * (len(operands) - left),
            out_specs=[vmem] * len(outs),
            scratch_shapes=list(scratch),
        ),
        compiler_params=pltpu.CompilerParams(vmem_limit_bytes=8 * MIB),
        cost_estimate=pl.CostEstimate(flops=flops, bytes_accessed=moved, transcendentals=0),
    )(*scalars, *operands[:left], *[fast(v) for v in operands[left:]])


def slow(v):
    return pltpu.with_memory_space_constraint(v, pltpu.HBM)


def block(i):
    return pl.ds(pl.multiple_of(i * BS, BS), BS)


def q_kernel(src, dst, live, stored, ids, out, adj, acc, sems):
    parts = sems.shape[0]
    n = adj.shape[0] // parts
    copies = [pltpu.make_async_copy(stored.at[pl.ds(i * n, n)], adj.at[pl.ds(i * n, n)], sems.at[i]) for i in range(parts)]
    for copy in copies:
        copy.start()
    acc[...] = jnp.zeros_like(acc)
    for part, copy in enumerate(copies):
        copy.wait()

        def step(i, carry):
            for u in range(Q_UNROLL):
                k = part * n + i * Q_UNROLL + u
                acc[:, block(src[k])] += dot(onehot_of(ids[dst[k]]), adj[k])
            return carry

        here = jnp.clip(live[0] - part * n, 0, n)
        lax.fori_loop(0, (here + Q_UNROLL - 1) // Q_UNROLL, step, 0)
    hi, lo = split(acc[:, : out.shape[1]])
    out[0:VN] = hi
    out[VN : 2 * VN] = lo


def source_kernel(q, *refs):
    shards, (panel, pool) = refs[:8], refs[8:]
    nodes = shards[0].shape[0]
    for spot, ref in enumerate(shards):
        panel[pl.ds(spot * nodes, nodes)] = ref[...]
    panel[pl.ds(8 * nodes, BS)] = jnp.zeros((BS, panel.shape[1]), BF16)
    total = jnp.zeros((2 * VN, panel.shape[1]), F32)
    deep = 1024
    for i in range(q.shape[1] // deep):
        rows = pl.ds(i * deep, deep)
        total += dot(q[0 : 2 * VN, rows], panel[rows])
    pool[...] = total[:VN] + total[VN:]


def target_kernel(adj, *refs):
    shards, near, far, (panel, adj_out, sem, sems) = refs[:8], refs[8], refs[9:12], refs[12:]
    load = pltpu.make_async_copy(adj, adj_out, sem)
    load.start()
    nodes = shards[0].shape[0]
    moves = [(ref, 0, spot, 1) for spot, ref in enumerate(shards)] + [(near, 0, 8, 5)]
    moves += [(ref, 0, 13 + i, 1) for i, ref in enumerate(far)]
    copies = []
    for ref, at, spot, n in moves:
        to = panel.at[pl.ds(spot * nodes, n * nodes)]
        copies.append(pltpu.make_async_copy(ref.at[pl.ds(at, n * nodes)], to, sems.at[len(copies)]))
    for copy in copies:
        copy.start()
    panel[pl.ds(16 * nodes, BS)] = jnp.zeros((BS, panel.shape[1]), BF16)
    for copy in copies:
        copy.wait()
    load.wait()


def final_kernel(gp, *refs):
    terms, out = refs[:-1], refs[-1]
    hi, lo = split(gp[...])
    nodes = out.shape[0]
    width = out.shape[1]
    for k in range(nodes // width):
        rows, ride = pl.ds(k * width, width), pl.ds(nodes + k * VN, VN)
        q = plus(*[t[ride] for t in terms]).astype(BF16)
        out[rows] = plus(*[t[rows] for t in terms]) + dot(q, hi, 0, 0) + dot(q, lo, 0, 0)


def pairs_kernel(backward, low, high, c0, c1, to, ends, adj, panel, *refs):
    width = panel.shape[1]
    zero = panel.shape[0] // BS - 1
    first_pair, last = ends[low], ends[high]
    out = refs[-1]
    begin = low * (out.shape[0] // BS // (high - low))

    def step(i, acc):
        for u in range(UNROLL):
            p = first_pair + i * UNROLL + u
            real = p < last
            p = jnp.minimum(p, last - 1)
            e0, e1, t = c0[p], c1[p], to[p]
            x0 = panel[block(jnp.where(real, e0 & 255, zero))]
            x1 = panel[block(jnp.where(real, e1 & 255, zero))]
            side = 0 if backward else 1
            lhs = jnp.concatenate([adj[e0 >> 8], adj[e1 >> 8]], axis=side)
            prod = dot(lhs, jnp.concatenate([x0, x1], axis=0), side, 0)
            fresh = jnp.logical_and(real, (t & 1) == 1)
            acc = prod + jnp.where(fresh, jnp.zeros_like(acc), acc)
            out[block((t >> 1) - begin)] = acc.astype(BF16)
        return acc

    steps = (last - first_pair + UNROLL - 1) // UNROLL
    lax.fori_loop(0, steps, step, jnp.zeros((BS, width), F32))
    if backward:
        q, pieces = refs[0], refs[1:-1]
        nodes = out.shape[0] // 4
        for spot, piece in enumerate(pieces):
            piece[pl.ds(0, nodes)] = out[pl.ds(spot * nodes, nodes)]
            for k in range(nodes // width):
                piece[pl.ds(nodes + k * VN, VN)] = q[0:VN, pl.ds(((low * 4 + spot) * 4 + k) * width, width)]


def plan(used, to, frm, n_to, zero, parts):
    kslots = used.shape[0]
    n_pairs = kslots // 2 + n_to
    k = jnp.arange(kslots)
    key = jnp.where(used, to, -1)
    d = jnp.arange(n_to)
    rank = jnp.sum((key[:, None] == key[None, :]) & (k[None, :] < k[:, None]), axis=1)
    count = jnp.sum(key[None, :] == d[:, None], axis=1)
    need = jnp.maximum(1, (count + 1) // 2)
    offset = jnp.sum(jnp.where(d[None, :] < d[:, None], need[None, :], 0), axis=1)
    base = jnp.sum(jnp.where(key[:, None] == d[None, :], offset[None, :], 0), axis=1)
    spot = jnp.where(used, 2 * base + rank, -1)
    p = jnp.arange(2 * n_pairs)
    code = zero + jnp.sum(jnp.where(p[:, None] == spot[None, :], (k * 256 + frm - zero)[None, :], 0), axis=1)
    code = code.reshape(n_pairs, 2).astype(jnp.int32)
    p = jnp.arange(n_pairs)
    at = jnp.sum(offset[None, :] <= p[:, None], axis=1) - 1
    first = jnp.sum(offset[None, :] == p[:, None], axis=1)
    ends = jnp.stack([offset[i * n_to // parts] for i in range(parts)] + [jnp.sum(need)]).astype(jnp.int32)
    return code[:, 0], code[:, 1], (2 * at + first).astype(jnp.int32), ends


def mlp_kernel(ids, pooled, w_in, w_out, cot, *refs):
    terms, (mixed_out, hidden_out, grad_pre_out, grad, pool) = refs[:5], refs[5:]
    p_hi, p_lo = split(pooled[...])
    tile = 256
    total = jnp.zeros(pooled.shape, F32)
    for i in range(cot.shape[0] // tile):
        rows = pl.ds(i * tile, tile)
        hot = onehot_of(ids[:, rows])
        spread = dot(hot, p_hi, 0, 0) + dot(hot, p_lo, 0, 0)
        mixed = (plus(*[t[rows] for t in terms]) + spread).astype(BF16)
        pre = dot(mixed, w_in[...])
        sig = jax.nn.sigmoid(pre)
        hidden_out[rows] = (pre * sig).astype(BF16)
        grad_hidden = dot(cot[rows], w_out[...], 1, 1)
        grad_pre = (grad_hidden * sig * (1.0 + pre * (1.0 - sig))).astype(BF16)
        hi, lo = split(dot(grad_pre, w_in[...], 1, 1) + cot[rows].astype(F32))
        total += dot(hot, hi) + dot(hot, lo)
        grad[rows] = hi
        mixed_out[rows] = mixed
        grad_pre_out[rows] = grad_pre
    pool[pl.ds(0, VN)], pool[pl.ds(VN, VN)] = split(total)


def mlp(vid, pooled, w_in, w_out, cot, parts):
    rows, width = cot.shape
    hidden = w_in.shape[1]
    return call(
        mlp_kernel, (), [vid, pooled, w_in, w_out, cot, *parts],
        [((rows, width), BF16), ((rows, hidden), BF16), ((rows, hidden), BF16), ((rows, width), BF16), ((2 * VN, width), BF16)],
        (), 6 * rows * width * hidden, 8 * rows * width,
    )


def shards(features, adj_w, row_of, col_of, live, vid, w_in, w_out, cotangent):
    adj = adj_w[0, 0]
    kslots = adj.shape[0]
    nodes, width = features.shape[1:]
    owned = nodes // BS
    scale = math.sqrt(VN / (nodes * 128))
    y, zh, x, zl, core = place()
    used = jnp.arange(kslots) < live[0, 0]
    tgt, src = row_of[0, 0], col_of[0, 0]
    far = tgt // owned
    near = (((far % 2) ^ core) * 2 + ((far // 8) ^ zl)) * 4 + (far // 2 - x) % 4
    dst_blocks = 16 * owned
    src_blocks = 8 * owned
    dst = jnp.where(used, near * owned + tgt % owned, dst_blocks).astype(jnp.int32)
    home = src // owned
    at = (((home // 4) ^ zh) * 4 + (home - y) % 4) * owned + src % owned
    src = jnp.where(used, at, src_blocks).astype(jnp.int32)
    tgt_read = jnp.where(used, tgt, 0)
    count = live[0]
    to_dst = plan(used, dst, src, dst_blocks, src_blocks, 4)
    to_src = plan(used, src, dst, src_blocks, dst_blocks, 2)
    part = width
    flops = 2 * kslots * BS * BS * part

    ring, pair = along("row")
    own, a1, a2, a3, b0 = gather_first("row", features[0])
    stored = slow(adj)
    ids = merge(merge(vid[0][None], "core", core), "x", x, 1)
    ids = merge(merge(ids, "x", x, 2), "zl", zl).reshape(dst_blocks, 1, BS)
    a2, ids = tie((a2, ids))
    b1, b2, b3 = ring(b0, -1), pair(a2), ring(b0, 1)
    ids = tie(ids, to_dst, to_src)
    q, adj = call(
        q_kernel, (src, tgt_read, count), [stored, ids], [((2 * VN, src_blocks * BS), BF16), (adj.shape, BF16)],
        [pltpu.VMEM((VN, (src_blocks + 1) * BS), F32), pltpu.SemaphoreType.DMA((5,))],
        2 * kslots * BS * BS * VN, adj.size * 2, 1,
    )
    pieces = [own, a1, a2, a3, b0, *tie((b1, b2, b3), q)]
    panel, pool = call(
        source_kernel, (), [q, *pieces], [(((src_blocks + 1) * BS, part), BF16), ((VN, part), F32)]
    )

    def forward(low, high, panel):
        return call(
            functools.partial(pairs_kernel, False, low, high), to_dst, [adj, panel],
            [((dst_blocks // 4 * (high - low) * BS, part), BF16)], (), flops // 2, adj.size,
        )[0]

    give = forward(2, 4, panel)
    pool, panel = tie((add(pool, "zl"), panel), give)
    got = send(give, core=1)
    keep_o = forward(1, 2, panel)
    pool, keep_o = tie((add(pool, "zh"), keep_o))
    piece = lambda keep, at, i: plus(keep[i * nodes : i * nodes + nodes], got[(at + i) * nodes : (at + i + 1) * nodes]).astype(BF16)
    other = [piece(keep_o, 4, i) for i in range(4)]
    o = scatter_first("col", other)
    pool, panel = tie((pool, panel), other)
    keep_w = forward(0, 1, panel)
    pool, keep_w = tie((add(pool, "y"), keep_w))
    pool, keep_w, o = tie((add(add(pool, "y", 2), "core"), keep_w, o))
    rider = jnp.concatenate(split(pool))
    own = [jnp.concatenate([piece(keep_w, 0, i), rider]) for i in range(4)]
    parts = scatter_last("col", own, scatter_add(own, other, o))
    riders = [p[nodes:] for p in parts[:4]]
    pooled = scale * plus(*[r[:VN] for r in riders], *[r[VN:] for r in riders])

    mixed, hidden, grad_pre, grad, pool = mlp(vid, pooled, w_in, w_out, cotangent[0], parts)
    ring, pair = along("col")
    own, a1, a2, a3, b0 = gather_first("col", grad)
    weights = jnp.concatenate([dot(grad_pre, mixed, 0, 0), dot(hidden, cotangent[0], 0, 0)])
    layer_out = (dot(hidden, w_out) + mixed.astype(F32)).astype(BF16)
    fan = w_in.shape[1]
    weights, pool = agree(weights, as_held(pool.astype(F32))[1], layer_out, "zl")
    quads = weights.reshape(4, fan // 2, width)
    pool = jnp.concatenate(split(pool))
    w0, w1, w2, w3 = [lax.dynamic_index_in_dim(quads, (x + k) % 4, 0, keepdims=False).astype(BF16) for k in range(4)]
    b0 = tie(b0, layer_out)
    a2 = tie(a2, w2)
    b1 = ring(jnp.concatenate([b0, w3, pool]), -1)
    b3 = ring(jnp.concatenate([b0, w1, pool]), 1)
    b2 = pair(a2)
    near = send(jnp.concatenate([own, a1, a2, a3, b0]), core=1)
    terms = jnp.concatenate([w0, pool]), ring(jnp.concatenate([w2, pool]), 2), b1[nodes:], b3[nodes:]
    terms = as_sent(*as_held(plus(*terms)))
    far = [send(b, core=1) for b in (b1, jnp.concatenate([b2, terms]), b3)]
    weights, pool = as_held(plus(terms, far[1][nodes:]))
    panel, adj = call(
        target_kernel, (), [stored, own, a1, a2, a3, b0, b1, b2, b3, near, *far],
        [(((dst_blocks + 1) * BS, part), BF16), (stored.shape, BF16)],
        [pltpu.SemaphoreType.DMA, pltpu.SemaphoreType.DMA((12,))], 0, stored.size * 2, 13,
    )
    weights, pool, panel = tie((*agree(weights, pool, panel, "y", 2), panel))

    ride = nodes // width * VN
    outs = [((nodes + ride, part), BF16)] * 4

    def backward(low, panel):
        return call(
            functools.partial(pairs_kernel, True, low, low + 1), to_src, [adj, panel, q],
            outs, [pltpu.VMEM((src_blocks // 2 * BS, part), BF16)], flops // 2, adj.size,
        )

    other = backward(1, panel)
    weights, pool, other = tie((*agree(weights, pool, other, "y"), other))
    o = scatter_first("row", other)
    own = backward(0, panel)
    own, o = tie((own, o))
    terms = scatter_last("row", own, scatter_add(own, other, o))
    weights, pool = agree(weights, pool, terms[-1], "zh")
    weights = weights.astype(BF16)
    for bit in (1, 2):
        weights = merge(weights, "x", x, bit)
    grad_in = weights[:fan].astype(F32).T
    grad_out = weights[fan:].astype(F32)
    grad_features = pl.pallas_call(
        final_kernel, out_shape=jax.ShapeDtypeStruct((nodes, part), F32)
    )(scale * pool, *[fast(t) for t in terms])
    return (layer_out[None], grad_features[None], grad_in, grad_out)


def solution(mesh):
    in_specs = (
        P("col", "row", None),
        P("row", "col", None, None, None),
        P("row", "col", None),
        P("row", "col", None),
        P("row", "col"),
        P("row", "col"),
        P(),
        P(),
        P("row", "col", None),
    )
    out_specs = (P("row", "col", None), P("col", "row", None), P(), P())
    return jax.shard_map(shards, mesh=mesh, in_specs=in_specs, out_specs=out_specs, check_vma=False)
```
